32 devices in a mesh: dp: 4 (over x, core), expert: 8 (over z, y).
Axes of the slice: x: 2, y: 2, z: 4, core: 2. Of those that a mesh axis runs over, the one named last changes fastest.
Arguments:
- tokens: bfloat16 [4096, 5120], P(('dp', 'expert')), may hold values from -6 to 6
- cotangent: bfloat16 [4096, 5120], P(('dp', 'expert')), may hold values from -6 to 6
- gate: float32 [4096], P(('dp', 'expert')), may hold values from 0.25 to 2
- clade: int32 [4096], P(('dp', 'expert')), may hold values from 0 to 7
- block: int32 [4096], P(('dp', 'expert')), may hold values from 0 to 20, as said below
- plan: int32 [8], replicated, may hold values from 0 to 7, as said below
- w_gu: bfloat16 [8, 2, 1408, 5120], P('expert', None, 'dp'), may hold values from -0.078125 to 0.078125
- w_down: bfloat16 [8, 1408, 5120], P('expert', 'dp'), may hold values from -0.15625 to 0.15625
Outputs:
- grad_tokens: bfloat16 [4096, 5120], P(('dp', 'expert'))
- grad_gu: bfloat16 [8, 2, 1408, 5120], P('expert', None, 'dp')
- grad_down: bfloat16 [8, 1408, 5120], P('expert', 'dp')
The draws below stay inside these ranges and needn't reach their ends.
Inputs may be any that keep to these rules, and one draw needn't show every extreme that they name: plan[e] is e (no replica) or (e + 4) mod 8; experts 0, 3, 4 and 7 always have a replica. A value below 16 places the token in its owner's block, 16 to 19 in its replica's block (only for experts with a replica), 20 drops it; among the 128 tokens of one device, tokens of the same clade have distinct values below 20.
All inputs are finite; a program needn't handle non-finite values.
Results may differ from the reference program's by a relative error of at most 0.0066.
Values may be sent and summed in bfloat16 or wider, within the bound.
A program may use at most 192 MiB of HBM per device.

```python
import math
import jax
import jax.numpy as jnp
from jax import lax

D = 5120
FF = 1408
TOK_DEV = 128
EXPERTS = 8
TOKENS = 4096
CAP_H = 16
CAP_G = 4
CAP = 20
N_DP = 4
N_EXPERT = 8
DEVICES = 32


def routing(key):
    half_way = EXPERTS // 2
    key_pick, key_tokens = jax.random.split(key, 2)
    every = jnp.arange(EXPERTS, dtype=jnp.int32)
    replicated = jax.random.randint(key_pick, (EXPERTS,), 0, 4) != 0
    forced = (every == 0) | (every == half_way - 1) | (every == half_way) | (every == EXPERTS - 1)
    replicated = replicated | forced
    plan = jnp.where(replicated, (every + half_way) % EXPERTS, every).astype(jnp.int32)
    cumul = jnp.cumsum(jnp.where(replicated, 3, 1)).astype(jnp.int32)
    picks = jax.random.randint(key_tokens, (TOKENS,), 0, cumul[EXPERTS - 1])
    clade = jnp.sum((picks[:, None] >= cumul[None, :]).astype(jnp.int32), axis=1).astype(jnp.int32)
    grouped = clade.reshape(TOKENS // TOK_DEV, TOK_DEV)
    member = (grouped[:, :, None] == every[None, None, :]).astype(jnp.int32)
    ranking = jnp.sum((jnp.cumsum(member, axis=1) - member) * member, axis=2).reshape(TOKENS)
    has_copy = replicated[clade]
    block = jnp.where(ranking < CAP_H, ranking, jnp.where(has_copy & (ranking < CAP), ranking, CAP))
    return (plan, clade, block.astype(jnp.int32))


def draw_clade(key, part):
    return routing(key)[1]


def draw_block(key, part):
    return routing(key)[2]


def draw_plan(key, part):
    return routing(key)[0]


def shard_levels(stream_key, extent, shards, smallest, top_value):
    gain = 1.0
    for dim, parts in shards:
        steps = jax.random.uniform(jax.random.fold_in(jax.random.fold_in(stream_key, 6), dim), (parts,), jnp.float32, smallest / len(shards), top_value / len(shards))
        gain = gain * jnp.repeat(jnp.exp(steps), extent[dim] // parts).reshape((-1,) + (1,) * (len(extent) - 1 - dim))
    return gain


def normal_values(own_key, dims, scale, bound, pieces=(), kind=jnp.bfloat16):
    loudness = shard_levels(own_key, dims, pieces, -0.22, 0.18) if pieces else 1.0
    entries = jax.random.normal(own_key, dims, jnp.float32) * scale * loudness
    return jnp.minimum(jnp.maximum(entries, -bound), bound).astype(kind)


def setup_inputs(seed: int = 0) -> dict:
    key_of = jax.random.split(jax.random.key(seed), 9)
    tokens = normal_values(key_of[0], (TOKENS, D), 1.0, 6.0, ((0, 32),))
    cotangent = normal_values(key_of[1], (TOKENS, D), 1.0, 6.0, ((0, 32),))
    gate = jnp.clip(jnp.exp(math.log(2.0) - 2.0794415 * jax.random.uniform(key_of[2], (TOKENS,), jnp.float32) ** shard_levels(key_of[2], (TOKENS,), ((0, 32),), -0.2, 0.2)), 0.25, 2.0)
    clade = draw_clade(jax.random.fold_in(key_of[8], 71), 0)
    block = draw_block(jax.random.fold_in(key_of[8], 71), 0)
    plan = draw_plan(jax.random.fold_in(key_of[8], 71), 0)
    w_gu = normal_values(key_of[6], (EXPERTS, 2, FF, D), D ** -0.5, 0.078125, ((0, 8), (2, 4)))
    w_down = normal_values(key_of[7], (EXPERTS, FF, D), FF ** -0.5, 0.15625, ((0, 8), (1, 4)))
    return dict(tokens=tokens, cotangent=cotangent, gate=gate, clade=clade, block=block, plan=plan, w_gu=w_gu, w_down=w_down)


def expert_pass(rows_x, rows_cot, gate_up, down_proj):
    gate_w = gate_up[0]
    up_w = gate_up[1]
    gate_pre = jnp.dot(rows_x, gate_w.T, preferred_element_type=jnp.float32)
    up_pre = jnp.dot(rows_x, up_w.T, preferred_element_type=jnp.float32)
    sigmoid = jax.nn.sigmoid(gate_pre)
    hidden = (gate_pre * sigmoid * up_pre).astype(jnp.bfloat16)
    hidden_cot = jnp.dot(rows_cot, down_proj.T, preferred_element_type=jnp.float32)
    up_cot = (hidden_cot * gate_pre * sigmoid).astype(jnp.bfloat16)
    gate_cot = (hidden_cot * up_pre * sigmoid * (1.0 + gate_pre * (1.0 - sigmoid))).astype(jnp.bfloat16)
    grads = jnp.stack([
        jnp.dot(gate_cot.T, rows_x, preferred_element_type=jnp.float32),
        jnp.dot(up_cot.T, rows_x, preferred_element_type=jnp.float32),
        jnp.dot(hidden.T, rows_cot, preferred_element_type=jnp.float32),
    ]).astype(jnp.bfloat16)
    row_count = rows_x.shape[0]
    slice_width = FF // N_DP
    gate_rows = gate_cot.astype(jnp.float32).reshape(row_count, N_DP, slice_width)
    up_rows = up_cot.astype(jnp.float32).reshape(row_count, N_DP, slice_width)
    gate_mat = gate_w.astype(jnp.float32).reshape(N_DP, slice_width, D)
    up_mat = up_w.astype(jnp.float32).reshape(N_DP, slice_width, D)
    partial_value = jnp.einsum("rkf,kfd->rkd", gate_rows, gate_mat, precision=lax.Precision.HIGHEST)
    partial_value = partial_value + jnp.einsum("rkf,kfd->rkd", up_rows, up_mat, precision=lax.Precision.HIGHEST)
    rounded = lax.optimization_barrier(partial_value.astype(jnp.bfloat16)).astype(jnp.float32)
    return grads, jnp.sum(rounded, axis=1).astype(jnp.bfloat16)


def reference(tokens, cotangent, gate, clade, block, plan, w_gu, w_down):
    half_way = N_EXPERT // 2
    scaled = (gate[:, None] * cotangent.astype(jnp.float32)).astype(jnp.bfloat16)
    index = jnp.arange(TOKENS, dtype=jnp.int32)
    source = (index // TOK_DEV).astype(jnp.int32)
    lookup = plan[clade]
    column = jnp.where(block < CAP_H, clade, lookup)
    kept = block < CAP
    slot = jnp.where(kept, column * CAP + block, N_EXPERT * CAP).astype(jnp.int32)
    table = jnp.full((DEVICES, N_EXPERT * CAP), TOKENS, jnp.int32)
    table = table.at[source, slot].set(index, mode="drop").reshape(DEVICES, N_EXPERT, CAP)
    padded_x = jnp.concatenate([tokens, jnp.zeros((1, D), jnp.bfloat16)], axis=0)
    padded_c = jnp.concatenate([scaled, jnp.zeros((1, D), jnp.bfloat16)], axis=0)

    def per_column(expert):
        partner = (expert + half_way) % N_EXPERT
        home_index = table[:, expert, :CAP_H].reshape(-1)
        guest_index = table[:, partner, CAP_H:].reshape(-1)
        home_grads, home_out = expert_pass(padded_x[home_index], padded_c[home_index], w_gu[expert], w_down[expert])
        guest_grads, guest_out = expert_pass(padded_x[guest_index], padded_c[guest_index], w_gu[expert], w_down[expert])
        total = (home_grads.astype(jnp.float32) + guest_grads.astype(jnp.float32)).astype(jnp.bfloat16)
        return total, home_out.reshape(DEVICES, CAP_H, D), guest_out.reshape(DEVICES, CAP_G, D)

    grads, home_rows, guest_rows = lax.map(per_column, jnp.arange(N_EXPERT, dtype=jnp.int32))
    guest_at = jnp.roll(guest_rows, half_way, axis=0)
    results = jnp.concatenate([home_rows, guest_at], axis=2)
    results = jnp.transpose(results, (1, 0, 2, 3)).reshape(DEVICES * N_EXPERT * CAP, D)
    flat = (source * (N_EXPERT * CAP) + jnp.where(kept, slot, 0)).astype(jnp.int32)
    grad_tokens = jnp.where(kept[:, None], results[flat], jnp.zeros((), jnp.bfloat16))
    return grad_tokens, grads[:, :2], grads[:, 2]
```

```python
import jax
import jax.numpy as jnp
from jax import lax
from jax.sharding import PartitionSpec as P


def routing(clade, block, plan, columns, cap_home, cap_rows):
    experts = plan.shape[0]
    matches = clade[:, None] == jnp.arange(experts, dtype=jnp.int32)[None, :]
    lookup = jnp.sum(jnp.where(matches, plan[None, :], 0), axis=1)
    owner = jnp.where(block < cap_home, clade, (lookup + columns // 2) % columns)
    return jnp.where(block < cap_rows, owner * cap_rows + block, -1)


def local(tokens, cotangent, gate, clade, block, plan, w_gu, w_down):
    columns = lax.axis_size("expert")
    tok_rows = tokens.shape[0]
    cap_home = tok_rows // columns
    cap_guest = tok_rows // (4 * columns)
    cap_rows = cap_home + cap_guest
    slot_count = columns * cap_rows
    slot = routing(clade, block, plan, columns, cap_home, cap_rows)
    selector = (jnp.arange(slot_count, dtype=jnp.int32)[:, None] == slot[None, :]).astype(
        jnp.bfloat16
    )
    f32 = jnp.float32
    bf16 = jnp.bfloat16
    scaled = (gate[:, None] * cotangent.astype(f32)).astype(bf16)
    send_x = jnp.dot(selector, tokens, preferred_element_type=f32).astype(bf16)
    send_c = jnp.dot(selector, scaled, preferred_element_type=f32).astype(bf16)

    def spread(rows):
        mine = lax.all_to_all(rows, "expert", split_axis=0, concat_axis=0, tiled=True)
        return lax.all_gather(mine, "dp", axis=0, tiled=True)

    rows_x = spread(send_x)
    rows_c = spread(send_c)
    contract_last = (((1,), (1,)), ((), ()))
    contract_rows = (((0,), (0,)), ((), ()))
    gate_w, up_w = w_gu[0, 0], w_gu[0, 1]
    down_w = w_down[0]
    gate_pre = lax.dot_general(rows_x, gate_w, contract_last, preferred_element_type=f32)
    up_pre = lax.dot_general(rows_x, up_w, contract_last, preferred_element_type=f32)
    hidden_cot = lax.dot_general(rows_c, down_w, contract_last, preferred_element_type=f32)
    sigmoid = jax.nn.sigmoid(gate_pre)
    hidden = (gate_pre * sigmoid * up_pre).astype(bf16)
    up_cot = (hidden_cot * gate_pre * sigmoid).astype(bf16)
    gate_cot = (hidden_cot * up_pre * sigmoid * (1.0 + gate_pre * (1.0 - sigmoid))).astype(bf16)
    part = jnp.dot(gate_cot, gate_w, preferred_element_type=f32)
    part = (part + jnp.dot(up_cot, up_w, preferred_element_type=f32)).astype(bf16)
    summed = lax.psum_scatter(part, "dp", scatter_dimension=0, tiled=True)
    result = lax.all_to_all(summed, "expert", split_axis=0, concat_axis=0, tiled=True)
    d_gate = lax.dot_general(gate_cot, rows_x, contract_rows, preferred_element_type=f32)
    d_up = lax.dot_general(up_cot, rows_x, contract_rows, preferred_element_type=f32)
    d_down = lax.dot_general(hidden, rows_c, contract_rows, preferred_element_type=f32)
    grad_gu = jnp.stack([d_gate.astype(bf16), d_up.astype(bf16)])[None]
    grad_tokens = lax.dot_general(selector, result, contract_rows, preferred_element_type=f32)
    return (grad_tokens.astype(bf16), grad_gu, d_down.astype(bf16)[None])


def solution(mesh):
    placed = (
        P(("dp", "expert"), None),
        P(("dp", "expert"), None),
        P(("dp", "expert")),
        P(("dp", "expert")),
        P(("dp", "expert")),
        P(),
        P("expert", None, "dp", None),
        P("expert", "dp", None),
    )
    return jax.shard_map(
        local,
        mesh=mesh,
        in_specs=placed,
        out_specs=(
            P(("dp", "expert"), None),
            P("expert", None, "dp", None),
            P("expert", "dp", None),
        ),
        check_vma=False,
    )
```

```python
import functools

import jax
import jax.numpy as jnp
from jax import lax
from jax.experimental import pallas as pl
from jax.experimental.pallas import tpu as pltpu
from jax.sharding import PartitionSpec as P

F32 = jnp.float32
BF16 = jnp.bfloat16
MESH = pl.DeviceIdType.MESH
LAST = (((1,), (1,)), ((), ()))
ROWS = (((0,), (0,)), ((), ()))


def one_hot(count, index):
    return (jnp.arange(count, dtype=jnp.int32)[:, None] == index[None, :]).astype(BF16)


def place(clade, block, plan, columns, cap_home):
    experts = plan.shape[0]
    matches = clade[:, None] == jnp.arange(experts, dtype=jnp.int32)[None, :]
    lookup = jnp.sum(jnp.where(matches, plan[None, :], 0), axis=1)
    return jnp.where(block < cap_home, clade, (lookup + columns // 2) % columns)


def visit_order(columns):
    half = columns // 2
    offsets = [half]
    for step in range(1, half):
        offsets += [step, half - step, columns - step, half + step]
    seen = []
    for offset in offsets:
        if offset not in seen:
            seen.append(offset)
    return [0] + seen


def peers(columns, groups):
    d = lax.axis_index("dp")
    e = lax.axis_index("expert")
    core = d + 1 - 2 * lax.rem(d, 2)
    across = lax.rem(d + 2, groups)
    return d, e, core, across, core + 2 - 4 * (core // 2)


def greet(d, e, core, across, columns):
    barrier = pltpu.get_barrier_semaphore()
    for j in range(1, columns):
        pl.semaphore_signal(
            barrier, inc=1, device_id=(d, lax.rem(e + j, columns)), device_id_type=MESH
        )
    pl.semaphore_signal(barrier, inc=1, device_id=(core, e), device_id_type=MESH)
    pl.semaphore_signal(barrier, inc=1, device_id=(across, e), device_id_type=MESH)
    pl.semaphore_wait(barrier, columns + 1)


def dispatch_kernel(columns, groups, *refs):
    sources = refs[:3]
    outs = refs[3:6]
    local_sem, send_a, send_core, send_x, send_fwd, recv = refs[6:]
    d, e, core, across, diagonal = peers(columns, groups)
    greet(d, e, core, across, columns)
    order = visit_order(columns)
    kinds = range(3)

    def rows(index):
        return pl.ds(pl.multiple_of(index * 16, 16), 16)

    def remote(k, source, slot, send_sem, target):
        return pltpu.make_async_remote_copy(
            src_ref=source,
            dst_ref=outs[k].at[rows(slot)],
            send_sem=send_sem,
            recv_sem=recv.at[slot, k],
            device_id=target,
            device_id_type=MESH,
        )

    def arrived(k, slot):
        pltpu.make_async_copy(outs[k].at[rows(slot)], outs[k].at[rows(slot)], recv.at[slot, k]).wait()

    copies = []
    local = []
    mine = d * columns + e
    for k in kinds:
        own = sources[k].at[rows(e)]
        copies.append(remote(k, own, mine, send_x.at[0, k], (across, e)))
        copies[-1].start()
        target = lax.rem(e + order[1], columns)
        copies.append(remote(k, sources[k].at[rows(target)], mine, send_a.at[1, k], (d, target)))
        copies[-1].start()
        copies.append(remote(k, own, mine, send_core.at[0, k], (core, e)))
        copies[-1].start()
    for i in range(2, columns):
        target = lax.rem(e + order[i], columns)
        for k in kinds:
            copies.append(remote(k, sources[k].at[rows(target)], mine, send_a.at[i, k], (d, target)))
            copies[-1].start()
    for k in kinds:
        copy = pltpu.make_async_copy(sources[k].at[rows(e)], outs[k].at[rows(mine)], local_sem.at[k])
        copy.start()
        local.append(copy)
    for i in range(columns + 1):
        if 0 < i < columns:
            slot = d * columns + lax.rem(e + columns - order[i], columns)
            for k in kinds:
                arrived(k, slot)
                block = outs[k].at[rows(slot)]
                copies.append(remote(k, block, slot, send_x.at[i, k], (across, e)))
                copies[-1].start()
                copies.append(remote(k, block, slot, send_core.at[i, k], (core, e)))
                copies[-1].start()
        if i > 0:
            slot = across * columns + lax.rem(e + columns - order[i - 1], columns)
            for k in kinds:
                arrived(k, slot)
                block = outs[k].at[rows(slot)]
                copies.append(remote(k, block, slot, send_fwd.at[i - 1, k], (core, e)))
                copies[-1].start()
    for group in (core, diagonal):
        for i in range(columns):
            slot = group * columns + lax.rem(e + columns - order[i], columns)
            for k in kinds:
                arrived(k, slot)
    for copy in local:
        copy.wait()
    for copy in copies:
        copy.wait_send()


def dispatch(send_x, send_c, send_g, columns, groups, row_count):
    width = send_x.shape[1]
    senders = columns * groups
    sem = pltpu.SemaphoreType.DMA
    return pl.pallas_call(
        functools.partial(dispatch_kernel, columns, groups),
        out_shape=(
            jax.ShapeDtypeStruct((row_count, width), BF16),
            jax.ShapeDtypeStruct((row_count, width), BF16),
            jax.ShapeDtypeStruct((senders * 16, width // 2), BF16),
        ),
        in_specs=[pl.BlockSpec(memory_space=pl.ANY)] * 3,
        out_specs=(pl.BlockSpec(memory_space=pl.ANY),) * 3,
        scratch_shapes=[
            sem((3,)),
            sem((columns, 3)),
            sem((columns, 3)),
            sem((columns, 3)),
            sem((columns, 3)),
            sem((senders, 3)),
        ],
        compiler_params=pltpu.CompilerParams(collective_id=0, has_side_effects=True),
        name="dispatch",
    )(send_x, send_c, send_g)


def return_kernel(columns, groups, part_h, part_g, out_h, out_g, *scratch):
    pair_in = scratch[0:2]
    pair_out = scratch[2:4]
    cross_in = scratch[4:6]
    final = scratch[6:8]
    send_core, send_x, send_a, recv_core, recv_x, recv_a = scratch[8:]
    parts = (part_h, part_g)
    outs = (out_h, out_g)
    d, e, core, across, diagonal = peers(columns, groups)
    greet(d, e, core, across, columns)
    order = visit_order(columns)
    order = order[1:] + [0]
    kinds = range(2)

    def rows(index):
        return pl.ds(pl.multiple_of(index * 16, 16), 16)

    copies = []
    core_in = {}
    for i in range(columns):
        s = lax.rem(e + order[i], columns)
        for side, group in ((0, diagonal), (1, core)):
            for k in kinds:
                place_in = pair_in[k].at[rows(side * columns + s)]
                copy = pltpu.make_async_remote_copy(
                    src_ref=parts[k].at[rows(group * columns + s)],
                    dst_ref=place_in,
                    send_sem=send_core.at[side, i, k],
                    recv_sem=recv_core.at[side, i, k],
                    device_id=(core, e),
                    device_id_type=MESH,
                )
                copy.start()
                copies.append(copy)
                core_in[side, i, k] = copy

    def add(a, b):
        return (a[...].astype(F32) + b[...].astype(F32)).astype(BF16)

    cross = {}
    back = {}

    def finish(i):
        s = lax.rem(e + order[i], columns)
        for k in kinds:
            core_in[1, i, k].wait_recv()
            cross[i, k].wait_recv()
            final[k][rows(s)] = (
                parts[k][rows(d * columns + s)].astype(F32)
                + pair_in[k][rows(columns + s)].astype(F32)
                + cross_in[k][rows(s)].astype(F32)
            ).astype(BF16)
            if i == columns - 1:
                outs[k][rows(e)] = final[k][rows(s)]
            else:
                copy = pltpu.make_async_remote_copy(
                    src_ref=final[k].at[rows(s)],
                    dst_ref=outs[k].at[rows(e)],
                    send_sem=send_a.at[i, k],
                    recv_sem=recv_a.at[i, k],
                    device_id=(d, s),
                    device_id_type=MESH,
                )
                copy.start()
                copies.append(copy)
                back[i, k] = copy

    for i in range(columns):
        s = lax.rem(e + order[i], columns)
        for k in kinds:
            core_in[0, i, k].wait_recv()
            pair_out[k][rows(s)] = (
                parts[k][rows(across * columns + s)].astype(F32)
                + pair_in[k][rows(s)].astype(F32)
            ).astype(BF16)
            copy = pltpu.make_async_remote_copy(
                src_ref=pair_out[k].at[rows(s)],
                dst_ref=cross_in[k].at[rows(s)],
                send_sem=send_x.at[i, k],
                recv_sem=recv_x.at[i, k],
                device_id=(across, e),
                device_id_type=MESH,
            )
            copy.start()
            copies.append(copy)
            cross[i, k] = copy
        if i >= 2:
            finish(i - 2)
    finish(columns - 2)
    finish(columns - 1)
    for copy in back.values():
        copy.wait_recv()
    for copy in copies:
        copy.wait_send()


def give_back(part, part_g, columns, groups):
    width = part.shape[1]
    thin = part_g.shape[1]
    sem = pltpu.SemaphoreType.DMA
    vmem = pl.BlockSpec(memory_space=pltpu.VMEM)
    scratch = []
    for count in (2 * columns, columns, columns, columns):
        for wide in (width, thin):
            scratch.append(pltpu.VMEM((count * 16, wide), BF16))
    return pl.pallas_call(
        functools.partial(return_kernel, columns, groups),
        out_shape=(
            jax.ShapeDtypeStruct((columns * 16, width), BF16),
            jax.ShapeDtypeStruct((columns * 16, thin), BF16),
        ),
        in_specs=[vmem, vmem],
        out_specs=(vmem, vmem),
        scratch_shapes=scratch
        + [
            sem((2, columns, 2)),
            sem((columns, 2)),
            sem((columns, 2)),
            sem((2, columns, 2)),
            sem((columns, 2)),
            sem((columns, 2)),
        ],
        compiler_params=pltpu.CompilerParams(
            collective_id=1, has_side_effects=True, vmem_limit_bytes=48 * 2**20
        ),
        name="give_back",
    )(part, part_g)


def expert_pass(rows_x, rows_c, w_gu, w_down, send_part):
    gate_w, up_w, down_w = w_gu[0, 0], w_gu[0, 1], w_down[0]
    gate_pre = lax.dot_general(rows_x, gate_w, LAST, preferred_element_type=F32)
    up_pre = lax.dot_general(rows_x, up_w, LAST, preferred_element_type=F32)
    hidden_cot = lax.dot_general(rows_c, down_w, LAST, preferred_element_type=F32)
    sigmoid = jax.nn.sigmoid(gate_pre)
    hidden = (gate_pre * sigmoid * up_pre).astype(BF16)
    up_cot = (hidden_cot * gate_pre * sigmoid).astype(BF16)
    gate_cot = (hidden_cot * up_pre * sigmoid * (1.0 + gate_pre * (1.0 - sigmoid))).astype(BF16)
    part = jnp.dot(gate_cot, gate_w, preferred_element_type=F32)
    part = (part + jnp.dot(up_cot, up_w, preferred_element_type=F32)).astype(BF16)
    result = send_part(part)
    d_gate = lax.dot_general(gate_cot, rows_x, ROWS, preferred_element_type=F32)
    d_up = lax.dot_general(up_cot, rows_x, ROWS, preferred_element_type=F32)
    d_down = lax.dot_general(hidden, rows_c, ROWS, preferred_element_type=F32)
    grad_gu = jnp.stack([d_gate.astype(BF16), d_up.astype(BF16)])[None]
    return result, grad_gu, d_down.astype(BF16)[None]


def pick(selector, rows):
    return jnp.dot(selector, rows, preferred_element_type=F32).astype(BF16)


def local_general(tokens, cotangent, gate, clade, block, plan, w_gu, w_down):
    columns = lax.axis_size("expert")
    cap_home = tokens.shape[0] // columns
    cap_rows = cap_home + tokens.shape[0] // (4 * columns)
    owner = place(clade, block, plan, columns, cap_home)
    slot = jnp.where(block < cap_rows, owner * cap_rows + block, -1)
    selector = one_hot(columns * cap_rows, slot)
    scaled = (gate[:, None] * cotangent.astype(F32)).astype(BF16)

    def spread(rows):
        mine = lax.all_to_all(rows, "expert", split_axis=0, concat_axis=0, tiled=True)
        return lax.all_gather(mine, "dp", axis=0, tiled=True)

    def send_part(part):
        summed = lax.psum_scatter(part, "dp", scatter_dimension=0, tiled=True)
        return lax.all_to_all(summed, "expert", split_axis=0, concat_axis=0, tiled=True)

    rows_x = spread(pick(selector, tokens))
    rows_c = spread(pick(selector, scaled))
    result, grad_gu, grad_down = expert_pass(rows_x, rows_c, w_gu, w_down, send_part)
    grad_tokens = lax.dot_general(selector, result, ROWS, preferred_element_type=F32)
    return grad_tokens.astype(BF16), grad_gu, grad_down


def local(tokens, cotangent, gate, clade, block, plan, w_gu, w_down):
    columns = lax.axis_size("expert")
    groups = lax.axis_size("dp")
    width = tokens.shape[1]
    cap_home = tokens.shape[0] // columns
    cap_guest = tokens.shape[0] // (4 * columns)
    senders = columns * groups
    owner = place(clade, block, plan, columns, cap_home)
    is_home = block < cap_home
    is_guest = (block >= cap_home) & (block < cap_home + cap_guest)
    sel_home = one_hot(columns * cap_home, jnp.where(is_home, owner * cap_home + block, -1))
    sel_guest = one_hot(
        columns * cap_guest, jnp.where(is_guest, owner * cap_guest + block - cap_home, -1)
    )
    scaled = (gate[:, None] * cotangent.astype(F32)).astype(BF16)
    guests = jnp.stack([pick(sel_guest, tokens), pick(sel_guest, scaled)])
    guests = guests.reshape(2, columns, cap_guest, 2, width // 2).transpose(1, 0, 3, 2, 4)
    guests = guests.reshape(columns * 4 * cap_guest, width // 2)
    home_rows = senders * cap_home
    rows_x, rows_c, got = dispatch(
        pick(sel_home, tokens),
        pick(sel_home, scaled),
        guests,
        columns,
        groups,
        home_rows + senders * cap_guest,
    )
    got = got.reshape(senders, 2, 2, cap_guest, width // 2).transpose(1, 0, 3, 2, 4)
    got = got.reshape(2, senders * cap_guest, width)
    rows_x = lax.dynamic_update_slice(rows_x, got[0], (home_rows, 0))
    rows_c = lax.dynamic_update_slice(rows_c, got[1], (home_rows, 0))

    def send_part(part):
        thin = part[home_rows:].reshape(senders, cap_guest, 4, width // 4).transpose(0, 2, 1, 3)
        return give_back(part, thin.reshape(senders * 4 * cap_guest, width // 4), columns, groups)

    (home, thin), grad_gu, grad_down = expert_pass(rows_x, rows_c, w_gu, w_down, send_part)
    thin = thin.reshape(columns, 4, cap_guest, width // 4).transpose(0, 2, 1, 3)
    thin = thin.reshape(columns * cap_guest, width)
    result = lax.dot_general(sel_home, home, ROWS, preferred_element_type=F32)
    result = result + lax.dot_general(sel_guest, thin, ROWS, preferred_element_type=F32)
    return result.astype(BF16), grad_gu, grad_down


def solution(mesh):
    placed = (
        P(("dp", "expert"), None),
        P(("dp", "expert"), None),
        P(("dp", "expert")),
        P(("dp", "expert")),
        P(("dp", "expert")),
        P(),
        P("expert", None, "dp", None),
        P("expert", "dp", None),
    )

    def run(*arrays):
        columns = mesh.shape["expert"]
        each = arrays[0].shape[0] // mesh.size
        whole_blocks = each == 16 * columns and mesh.shape["dp"] == 4
        return jax.shard_map(
            local if whole_blocks else local_general,
            mesh=mesh,
            in_specs=placed,
            out_specs=(
                P(("dp", "expert"), None),
                P("expert", None, "dp", None),
                P("expert", "dp", None),
            ),
            check_vma=False,
        )(*arrays)

    return run
```

```python
import functools

import jax
import jax.numpy as jnp
from jax import lax
from jax.experimental import pallas as pl
from jax.experimental.pallas import tpu as pltpu
from jax.sharding import PartitionSpec as P

F32 = jnp.float32
BF16 = jnp.bfloat16
MESH = pl.DeviceIdType.MESH
LAST = (((1,), (1,)), ((), ()))
ROWS = (((0,), (0,)), ((), ()))


def one_hot(count, index):
    return (jnp.arange(count, dtype=jnp.int32)[:, None] == index[None, :]).astype(BF16)


def place(clade, block, plan, columns, cap_home):
    experts = plan.shape[0]
    matches = clade[:, None] == jnp.arange(experts, dtype=jnp.int32)[None, :]
    lookup = jnp.sum(jnp.where(matches, plan[None, :], 0), axis=1)
    return jnp.where(block < cap_home, clade, (lookup + columns // 2) % columns)


def flipped(index, mask, columns):
    total = 0
    bit = 1
    while bit < columns:
        total = total + lax.rem(lax.div(index, bit) + (mask // bit) % 2, 2) * bit
        bit *= 2
    return total


def peers(columns, groups):
    d = lax.axis_index("dp")
    e = lax.axis_index("expert")
    core = d + 1 - 2 * lax.rem(d, 2)
    across = lax.rem(d + 2, groups)
    return d, e, core, across, core + 2 - 4 * (core // 2)


def greet(d, e, core, across, columns):
    barrier = pltpu.get_barrier_semaphore()
    for mask in range(1, columns):
        pl.semaphore_signal(
            barrier, inc=1, device_id=(d, flipped(e, mask, columns)), device_id_type=MESH
        )
    pl.semaphore_signal(barrier, inc=1, device_id=(core, e), device_id_type=MESH)
    pl.semaphore_signal(barrier, inc=1, device_id=(across, e), device_id_type=MESH)
    pl.semaphore_wait(barrier, columns + 1)


def dispatch_kernel(columns, groups, *refs):
    sources = refs[:3]
    outs = refs[3:6]
    local_sem, send_a, send_core, send_x, send_fwd, recv = refs[6:]
    d, e, core, across, diagonal = peers(columns, groups)
    greet(d, e, core, across, columns)
    half = columns // 2
    near = [flipped(e, mask, columns) for mask in range(columns)]
    sends = [mask for pair in zip(range(1, half + 1), range(half, columns)) for mask in pair]
    sends = list(dict.fromkeys(sends))
    kinds = range(3)

    def rows(index):
        return pl.ds(pl.multiple_of(index * 16, 16), 16)

    def remote(k, source, slot, send_sem, target):
        return pltpu.make_async_remote_copy(
            src_ref=source,
            dst_ref=outs[k].at[rows(slot)],
            send_sem=send_sem,
            recv_sem=recv.at[slot, k],
            device_id=target,
            device_id_type=MESH,
        )

    def arrived(k, slot):
        pltpu.make_async_copy(outs[k].at[rows(slot)], outs[k].at[rows(slot)], recv.at[slot, k]).wait()

    copies = []
    local = []
    mine = d * columns + e
    for k in kinds:
        own = sources[k].at[rows(e)]
        copies.append(remote(k, own, mine, send_x.at[0, k], (across, e)))
        copies[-1].start()
    for mask in sends:
        target = near[mask]
        for k in kinds:
            source = sources[k].at[rows(target)]
            copies.append(remote(k, source, mine, send_a.at[mask, k], (d, target)))
            copies[-1].start()
    for k in kinds:
        own = sources[k].at[rows(e)]
        copies.append(remote(k, own, mine, send_core.at[0, k], (core, e)))
        copies[-1].start()
    for k in kinds:
        copy = pltpu.make_async_copy(sources[k].at[rows(e)], outs[k].at[rows(mine)], local_sem.at[k])
        copy.start()
        local.append(copy)
    for i in range(columns + 2):
        if 0 < i < columns:
            slot = d * columns + near[i]
            for k in kinds:
                arrived(k, slot)
                block = outs[k].at[rows(slot)]
                copies.append(remote(k, block, slot, send_x.at[i, k], (across, e)))
                copies[-1].start()
                copies.append(remote(k, block, slot, send_core.at[i, k], (core, e)))
                copies[-1].start()
        if i > 1:
            slot = across * columns + near[i - 2]
            for k in kinds:
                arrived(k, slot)
                block = outs[k].at[rows(slot)]
                copies.append(remote(k, block, slot, send_fwd.at[i - 2, k], (core, e)))
                copies[-1].start()
    for group in (core, diagonal):
        for i in range(columns):
            slot = group * columns + near[i]
            for k in kinds:
                arrived(k, slot)
    for copy in local:
        copy.wait()
    for copy in copies:
        copy.wait_send()


def dispatch(send_x, send_c, send_g, columns, groups, row_count):
    width = send_x.shape[1]
    senders = columns * groups
    sem = pltpu.SemaphoreType.DMA
    return pl.pallas_call(
        functools.partial(dispatch_kernel, columns, groups),
        out_shape=(
            jax.ShapeDtypeStruct((row_count, width), BF16),
            jax.ShapeDtypeStruct((row_count, width), BF16),
            jax.ShapeDtypeStruct((senders * 16, width // 2), BF16),
        ),
        in_specs=[pl.BlockSpec(memory_space=pl.ANY)] * 3,
        out_specs=(pl.BlockSpec(memory_space=pl.ANY),) * 3,
        scratch_shapes=[
            sem((3,)),
            sem((columns, 3)),
            sem((columns, 3)),
            sem((columns, 3)),
            sem((columns, 3)),
            sem((senders, 3)),
        ],
        compiler_params=pltpu.CompilerParams(collective_id=0, has_side_effects=True),
        name="dispatch",
    )(send_x, send_c, send_g)


def return_kernel(columns, groups, part_h, part_g, out_h, out_g, *scratch):
    pair_in = scratch[0:2]
    pair_out = scratch[2:4]
    cross_in = scratch[4:6]
    final = scratch[6:8]
    send_core, send_x, send_a, recv_core, recv_x, recv_a = scratch[8:]
    parts = (part_h, part_g)
    outs = (out_h, out_g)
    d, e, core, across, diagonal = peers(columns, groups)
    greet(d, e, core, across, columns)
    half = columns // 2
    order = list(range(half, columns)) + list(range(half - 1, -1, -1))
    order = [flipped(e, mask, columns) for mask in order]
    kinds = range(2)

    def rows(index):
        return pl.ds(pl.multiple_of(index * 16, 16), 16)

    copies = []
    core_in = {}
    for i in range(columns):
        s = order[i]
        for side, group in ((0, diagonal), (1, core)):
            for k in kinds:
                place_in = pair_in[k].at[rows(side * columns + s)]
                copy = pltpu.make_async_remote_copy(
                    src_ref=parts[k].at[rows(group * columns + s)],
                    dst_ref=place_in,
                    send_sem=send_core.at[side, i, k],
                    recv_sem=recv_core.at[side, i, k],
                    device_id=(core, e),
                    device_id_type=MESH,
                )
                copy.start()
                copies.append(copy)
                core_in[side, i, k] = copy

    cross = {}
    back = {}

    def finish(i):
        s = order[i]
        for k in kinds:
            core_in[1, i, k].wait_recv()
            cross[i, k].wait_recv()
            final[k][rows(s)] = (
                parts[k][rows(d * columns + s)].astype(F32)
                + pair_in[k][rows(columns + s)].astype(F32)
                + cross_in[k][rows(s)].astype(F32)
            ).astype(BF16)
            if i == columns - 1:
                outs[k][rows(e)] = final[k][rows(s)]
            else:
                copy = pltpu.make_async_remote_copy(
                    src_ref=final[k].at[rows(s)],
                    dst_ref=outs[k].at[rows(e)],
                    send_sem=send_a.at[i, k],
                    recv_sem=recv_a.at[i, k],
                    device_id=(d, s),
                    device_id_type=MESH,
                )
                copy.start()
                copies.append(copy)
                back[i, k] = copy

    for i in range(columns):
        s = order[i]
        for k in kinds:
            core_in[0, i, k].wait_recv()
            pair_out[k][rows(s)] = (
                parts[k][rows(across * columns + s)].astype(F32)
                + pair_in[k][rows(s)].astype(F32)
            ).astype(BF16)
            copy = pltpu.make_async_remote_copy(
                src_ref=pair_out[k].at[rows(s)],
                dst_ref=cross_in[k].at[rows(s)],
                send_sem=send_x.at[i, k],
                recv_sem=recv_x.at[i, k],
                device_id=(across, e),
                device_id_type=MESH,
            )
            copy.start()
            copies.append(copy)
            cross[i, k] = copy
        if i >= 2:
            finish(i - 2)
    finish(columns - 2)
    finish(columns - 1)
    for copy in back.values():
        copy.wait_recv()
    for copy in copies:
        copy.wait_send()


def give_back(part, part_g, columns, groups):
    width = part.shape[1]
    thin = part_g.shape[1]
    sem = pltpu.SemaphoreType.DMA
    vmem = pl.BlockSpec(memory_space=pltpu.VMEM)
    scratch = []
    for count in (2 * columns, columns, columns, columns):
        for wide in (width, thin):
            scratch.append(pltpu.VMEM((count * 16, wide), BF16))
    return pl.pallas_call(
        functools.partial(return_kernel, columns, groups),
        out_shape=(
            jax.ShapeDtypeStruct((columns * 16, width), BF16),
            jax.ShapeDtypeStruct((columns * 16, thin), BF16),
        ),
        in_specs=[vmem, vmem],
        out_specs=(vmem, vmem),
        scratch_shapes=scratch
        + [
            sem((2, columns, 2)),
            sem((columns, 2)),
            sem((columns, 2)),
            sem((2, columns, 2)),
            sem((columns, 2)),
            sem((columns, 2)),
        ],
        compiler_params=pltpu.CompilerParams(
            collective_id=1, has_side_effects=True, vmem_limit_bytes=48 * 2**20
        ),
        name="give_back",
    )(part, part_g)


def expert_pass(rows_x, rows_c, w_gu, w_down, send_part):
    units = w_gu.shape[2]
    both_w = w_gu.reshape(2 * units, w_gu.shape[3])
    pre = lax.dot_general(rows_x, both_w, LAST, preferred_element_type=F32)
    gate_pre, up_pre = pre[:, :units], pre[:, units:]
    hidden_cot = lax.dot_general(rows_c, w_down[0], LAST, preferred_element_type=F32)
    sigmoid = jax.nn.sigmoid(gate_pre)
    hidden = (gate_pre * sigmoid * up_pre).astype(BF16)
    up_cot = (hidden_cot * gate_pre * sigmoid).astype(BF16)
    gate_cot = (hidden_cot * up_pre * sigmoid * (1.0 + gate_pre * (1.0 - sigmoid))).astype(BF16)
    both_cot = jnp.concatenate([gate_cot, up_cot], axis=1)
    part = jnp.dot(both_cot, both_w, preferred_element_type=F32).astype(BF16)
    result = send_part(part)
    d_both = lax.dot_general(both_cot, rows_x, ROWS, preferred_element_type=F32)
    d_down = lax.dot_general(hidden, rows_c, ROWS, preferred_element_type=F32)
    return result, d_both.astype(BF16).reshape(w_gu.shape), d_down.astype(BF16)[None]


def pick(selector, rows):
    return jnp.dot(selector, rows, preferred_element_type=F32).astype(BF16)


def local_general(tokens, cotangent, gate, clade, block, plan, w_gu, w_down):
    columns = lax.axis_size("expert")
    cap_home = tokens.shape[0] // columns
    cap_rows = cap_home + tokens.shape[0] // (4 * columns)
    owner = place(clade, block, plan, columns, cap_home)
    slot = jnp.where(block < cap_rows, owner * cap_rows + block, -1)
    selector = one_hot(columns * cap_rows, slot)
    scaled = (gate[:, None] * cotangent.astype(F32)).astype(BF16)

    def spread(rows):
        mine = lax.all_to_all(rows, "expert", split_axis=0, concat_axis=0, tiled=True)
        return lax.all_gather(mine, "dp", axis=0, tiled=True)

    def send_part(part):
        summed = lax.psum_scatter(part, "dp", scatter_dimension=0, tiled=True)
        return lax.all_to_all(summed, "expert", split_axis=0, concat_axis=0, tiled=True)

    rows_x = spread(pick(selector, tokens))
    rows_c = spread(pick(selector, scaled))
    result, grad_gu, grad_down = expert_pass(rows_x, rows_c, w_gu, w_down, send_part)
    grad_tokens = lax.dot_general(selector, result, ROWS, preferred_element_type=F32)
    return grad_tokens.astype(BF16), grad_gu, grad_down


def local(tokens, cotangent, gate, clade, block, plan, w_gu, w_down):
    columns = lax.axis_size("expert")
    groups = lax.axis_size("dp")
    width = tokens.shape[1]
    cap_home = tokens.shape[0] // columns
    cap_guest = tokens.shape[0] // (4 * columns)
    senders = columns * groups
    owner = place(clade, block, plan, columns, cap_home)
    is_home = block < cap_home
    is_guest = (block >= cap_home) & (block < cap_home + cap_guest)
    sel_home = one_hot(columns * cap_home, jnp.where(is_home, owner * cap_home + block, -1))
    sel_guest = one_hot(
        columns * cap_guest, jnp.where(is_guest, owner * cap_guest + block - cap_home, -1)
    )
    scaled = (gate[:, None] * cotangent.astype(F32)).astype(BF16)
    guests = jnp.stack([pick(sel_guest, tokens), pick(sel_guest, scaled)])
    guests = guests.reshape(2, columns, cap_guest, 2, width // 2).transpose(1, 0, 3, 2, 4)
    guests = guests.reshape(columns * 4 * cap_guest, width // 2)
    home_rows = senders * cap_home
    rows_x, rows_c, got = dispatch(
        pick(sel_home, tokens),
        pick(sel_home, scaled),
        guests,
        columns,
        groups,
        home_rows + senders * cap_guest,
    )
    got = got.reshape(senders, 2, 2, cap_guest, width // 2).transpose(1, 0, 3, 2, 4)
    got = got.reshape(2, senders * cap_guest, width)
    rows_x = lax.dynamic_update_slice(rows_x, got[0], (home_rows, 0))
    rows_c = lax.dynamic_update_slice(rows_c, got[1], (home_rows, 0))

    def send_part(part):
        thin = part[home_rows:].reshape(senders, cap_guest, 4, width // 4).transpose(0, 2, 1, 3)
        return give_back(part, thin.reshape(senders * 4 * cap_guest, width // 4), columns, groups)

    (home, thin), grad_gu, grad_down = expert_pass(rows_x, rows_c, w_gu, w_down, send_part)
    thin = thin.reshape(columns, 4, cap_guest, width // 4).transpose(0, 2, 1, 3)
    thin = thin.reshape(columns * cap_guest, width)
    result = lax.dot_general(sel_home, home, ROWS, preferred_element_type=F32)
    result = result + lax.dot_general(sel_guest, thin, ROWS, preferred_element_type=F32)
    return result.astype(BF16), grad_gu, grad_down


def solution(mesh):
    placed = (
        P(("dp", "expert"), None),
        P(("dp", "expert"), None),
        P(("dp", "expert")),
        P(("dp", "expert")),
        P(("dp", "expert")),
        P(),
        P("expert", None, "dp", None),
        P("expert", "dp", None),
    )

    def run(*arrays):
        columns = mesh.shape["expert"]
        each = arrays[0].shape[0] // mesh.size
        whole_blocks = each == 16 * columns and mesh.shape["dp"] == 4
        return jax.shard_map(
            local if whole_blocks else local_general,
            mesh=mesh,
            in_specs=placed,
            out_specs=(
                P(("dp", "expert"), None),
                P("expert", None, "dp", None),
                P("expert", "dp", None),
            ),
            check_vma=False,
        )(*arrays)

    return run
```

```python
import functools

import jax
import jax.numpy as jnp
from jax import lax
from jax.experimental import pallas as pl
from jax.experimental.pallas import tpu as pltpu
from jax.sharding import PartitionSpec as P

F32 = jnp.float32
BF16 = jnp.bfloat16
MESH = pl.DeviceIdType.MESH
LAST = (((1,), (1,)), ((), ()))
ROWS = (((0,), (0,)), ((), ()))


def one_hot(count, index):
    return (jnp.arange(count, dtype=jnp.int32)[:, None] == index[None, :]).astype(BF16)


def place(clade, block, plan, columns, cap_home):
    experts = plan.shape[0]
    matches = clade[:, None] == jnp.arange(experts, dtype=jnp.int32)[None, :]
    lookup = jnp.sum(jnp.where(matches, plan[None, :], 0), axis=1)
    return jnp.where(block < cap_home, clade, (lookup + columns // 2) % columns)


def flipped(index, mask, columns):
    total = 0
    bit = 1
    while bit < columns:
        total = total + lax.rem(lax.div(index, bit) + (mask // bit) % 2, 2) * bit
        bit *= 2
    return total


def peers(columns, groups):
    d = lax.axis_index("dp")
    e = lax.axis_index("expert")
    core = d + 1 - 2 * lax.rem(d, 2)
    across = lax.rem(d + 2, groups)
    return d, e, core, across, core + 2 - 4 * (core // 2)


def greet(d, e, core, across, columns):
    barrier = pltpu.get_barrier_semaphore()
    for mask in range(1, columns):
        pl.semaphore_signal(
            barrier, inc=1, device_id=(d, flipped(e, mask, columns)), device_id_type=MESH
        )
    pl.semaphore_signal(barrier, inc=1, device_id=(core, e), device_id_type=MESH)
    pl.semaphore_signal(barrier, inc=1, device_id=(across, e), device_id_type=MESH)
    pl.semaphore_wait(barrier, columns + 1)


def dispatch_kernel(columns, groups, *refs):
    sources = refs[:3]
    outs = refs[3:6]
    local_sem, send_a, send_core, send_x, send_fwd, recv = refs[6:]
    d, e, core, across, diagonal = peers(columns, groups)
    greet(d, e, core, across, columns)
    half = columns // 2
    near = [flipped(e, mask, columns) for mask in range(columns)]
    sends = [mask for pair in zip(range(1, half + 1), range(half, columns)) for mask in pair]
    sends = list(dict.fromkeys(sends))
    kinds = range(3)

    def rows(index):
        return pl.ds(pl.multiple_of(index * 16, 16), 16)

    def remote(k, source, slot, send_sem, target):
        return pltpu.make_async_remote_copy(
            src_ref=source,
            dst_ref=outs[k].at[rows(slot)],
            send_sem=send_sem,
            recv_sem=recv.at[slot, k],
            device_id=target,
            device_id_type=MESH,
        )

    def arrived(k, slot):
        pltpu.make_async_copy(outs[k].at[rows(slot)], outs[k].at[rows(slot)], recv.at[slot, k]).wait()

    copies = []
    local = []
    mine = d * columns + e
    for k in kinds:
        own = sources[k].at[rows(e)]
        copies.append(remote(k, own, mine, send_x.at[0, k], (across, e)))
        copies[-1].start()
    for mask in sends:
        target = near[mask]
        for k in kinds:
            source = sources[k].at[rows(target)]
            copies.append(remote(k, source, mine, send_a.at[mask, k], (d, target)))
            copies[-1].start()
    for k in kinds:
        own = sources[k].at[rows(e)]
        copies.append(remote(k, own, mine, send_core.at[0, k], (core, e)))
        copies[-1].start()
    for k in kinds:
        copy = pltpu.make_async_copy(sources[k].at[rows(e)], outs[k].at[rows(mine)], local_sem.at[k])
        copy.start()
        local.append(copy)
    for i in range(columns + 2):
        if 0 < i < columns:
            slot = d * columns + near[i]
            for k in kinds:
                arrived(k, slot)
                block = outs[k].at[rows(slot)]
                copies.append(remote(k, block, slot, send_x.at[i, k], (across, e)))
                copies[-1].start()
                copies.append(remote(k, block, slot, send_core.at[i, k], (core, e)))
                copies[-1].start()
        if i > 1:
            slot = across * columns + near[i - 2]
            for k in kinds:
                arrived(k, slot)
                block = outs[k].at[rows(slot)]
                copies.append(remote(k, block, slot, send_fwd.at[i - 2, k], (core, e)))
                copies[-1].start()
    for group in (core, diagonal):
        for i in range(columns):
            slot = group * columns + near[i]
            for k in kinds:
                arrived(k, slot)
    for copy in local:
        copy.wait()
    for copy in copies:
        copy.wait_send()


def dispatch(send_x, send_c, send_g, columns, groups, row_count):
    width = send_x.shape[1]
    senders = columns * groups
    sem = pltpu.SemaphoreType.DMA
    return pl.pallas_call(
        functools.partial(dispatch_kernel, columns, groups),
        out_shape=(
            jax.ShapeDtypeStruct((row_count, width), BF16),
            jax.ShapeDtypeStruct((row_count, width), BF16),
            jax.ShapeDtypeStruct((senders * 16, width // 2), BF16),
        ),
        in_specs=[pl.BlockSpec(memory_space=pl.ANY)] * 3,
        out_specs=(pl.BlockSpec(memory_space=pl.ANY),) * 3,
        scratch_shapes=[
            sem((3,)),
            sem((columns, 3)),
            sem((columns, 3)),
            sem((columns, 3)),
            sem((columns, 3)),
            sem((senders, 3)),
        ],
        compiler_params=pltpu.CompilerParams(collective_id=0, has_side_effects=True),
        name="dispatch",
    )(send_x, send_c, send_g)


def return_kernel(columns, groups, part_h, part_g, out_h, out_g, *scratch):
    pair_in = scratch[0:2]
    pair_out = scratch[2:4]
    cross_in = scratch[4:6]
    final = scratch[6:8]
    send_core, send_x, send_a, recv_core, recv_x, recv_a = scratch[8:]
    parts = (part_h, part_g)
    outs = (out_h, out_g)
    d, e, core, across, diagonal = peers(columns, groups)
    greet(d, e, core, across, columns)
    half = columns // 2
    ahead = half
    order = list(range(half, columns)) + list(range(half - 1, -1, -1))
    order = [flipped(e, mask, columns) for mask in order]
    kinds = range(2)

    def rows(index):
        return pl.ds(pl.multiple_of(index * 16, 16), 16)

    copies = []
    core_in = {}
    for i in range(columns):
        s = order[i]
        for side, group in ((0, diagonal), (1, core)):
            for k in kinds:
                place_in = pair_in[k].at[rows(side * columns + s)]
                copy = pltpu.make_async_remote_copy(
                    src_ref=parts[k].at[rows(group * columns + s)],
                    dst_ref=place_in,
                    send_sem=send_core.at[side, i, k],
                    recv_sem=recv_core.at[side, i, k],
                    device_id=(core, e),
                    device_id_type=MESH,
                )
                copy.start()
                copies.append(copy)
                core_in[side, i, k] = copy

    cross = {}
    back = {}

    def finish(i):
        s = order[i]
        for k in kinds:
            core_in[1, i, k].wait_recv()
            cross[i, k].wait_recv()
            final[k][rows(s)] = (
                parts[k][rows(d * columns + s)].astype(F32)
                + pair_in[k][rows(columns + s)].astype(F32)
                + cross_in[k][rows(s)].astype(F32)
            ).astype(BF16)
            if i == columns - 1:
                outs[k][rows(e)] = final[k][rows(s)]
            else:
                copy = pltpu.make_async_remote_copy(
                    src_ref=final[k].at[rows(s)],
                    dst_ref=outs[k].at[rows(e)],
                    send_sem=send_a.at[i, k],
                    recv_sem=recv_a.at[i, k],
                    device_id=(d, s),
                    device_id_type=MESH,
                )
                copy.start()
                copies.append(copy)
                back[i, k] = copy

    for i in range(columns):
        s = order[i]
        for k in kinds:
            core_in[0, i, k].wait_recv()
            pair_out[k][rows(s)] = (
                parts[k][rows(across * columns + s)].astype(F32)
                + pair_in[k][rows(s)].astype(F32)
            ).astype(BF16)
            copy = pltpu.make_async_remote_copy(
                src_ref=pair_out[k].at[rows(s)],
                dst_ref=cross_in[k].at[rows(s)],
                send_sem=send_x.at[i, k],
                recv_sem=recv_x.at[i, k],
                device_id=(across, e),
                device_id_type=MESH,
            )
            copy.start()
            copies.append(copy)
            cross[i, k] = copy
        if i >= ahead:
            finish(i - ahead)
    for i in range(columns - ahead, columns):
        finish(i)
    for copy in back.values():
        copy.wait_recv()
    for copy in copies:
        copy.wait_send()


def give_back(part, part_g, columns, groups):
    width = part.shape[1]
    thin = part_g.shape[1]
    sem = pltpu.SemaphoreType.DMA
    vmem = pl.BlockSpec(memory_space=pltpu.VMEM)
    scratch = []
    for count in (2 * columns, columns, columns, columns):
        for wide in (width, thin):
            scratch.append(pltpu.VMEM((count * 16, wide), BF16))
    return pl.pallas_call(
        functools.partial(return_kernel, columns, groups),
        out_shape=(
            jax.ShapeDtypeStruct((columns * 16, width), BF16),
            jax.ShapeDtypeStruct((columns * 16, thin), BF16),
        ),
        in_specs=[vmem, vmem],
        out_specs=(vmem, vmem),
        scratch_shapes=scratch
        + [
            sem((2, columns, 2)),
            sem((columns, 2)),
            sem((columns, 2)),
            sem((2, columns, 2)),
            sem((columns, 2)),
            sem((columns, 2)),
        ],
        compiler_params=pltpu.CompilerParams(
            collective_id=1, has_side_effects=True, vmem_limit_bytes=48 * 2**20
        ),
        name="give_back",
    )(part, part_g)


def expert_pass(rows_x, rows_c, w_gu, w_down, send_part):
    units = w_gu.shape[2]
    both_w = w_gu.reshape(2 * units, w_gu.shape[3])
    pre = lax.dot_general(rows_x, both_w, LAST, preferred_element_type=F32)
    gate_pre, up_pre = pre[:, :units], pre[:, units:]
    hidden_cot = lax.dot_general(rows_c, w_down[0], LAST, preferred_element_type=F32)
    sigmoid = jax.nn.sigmoid(gate_pre)
    hidden = (gate_pre * sigmoid * up_pre).astype(BF16)
    up_cot = (hidden_cot * gate_pre * sigmoid).astype(BF16)
    gate_cot = (hidden_cot * up_pre * sigmoid * (1.0 + gate_pre * (1.0 - sigmoid))).astype(BF16)
    both_cot = jnp.concatenate([gate_cot, up_cot], axis=1)
    part = jnp.dot(both_cot, both_w, preferred_element_type=F32).astype(BF16)
    result = send_part(part)
    d_both = lax.dot_general(both_cot, rows_x, ROWS, preferred_element_type=F32)
    d_down = lax.dot_general(hidden, rows_c, ROWS, preferred_element_type=F32)
    return result, d_both.astype(BF16).reshape(w_gu.shape), d_down.astype(BF16)[None]


def pick(selector, rows):
    return jnp.dot(selector, rows, preferred_element_type=F32).astype(BF16)


def local_general(tokens, cotangent, gate, clade, block, plan, w_gu, w_down):
    columns = lax.axis_size("expert")
    cap_home = tokens.shape[0] // columns
    cap_rows = cap_home + tokens.shape[0] // (4 * columns)
    owner = place(clade, block, plan, columns, cap_home)
    slot = jnp.where(block < cap_rows, owner * cap_rows + block, -1)
    selector = one_hot(columns * cap_rows, slot)
    scaled = (gate[:, None] * cotangent.astype(F32)).astype(BF16)

    def spread(rows):
        mine = lax.all_to_all(rows, "expert", split_axis=0, concat_axis=0, tiled=True)
        return lax.all_gather(mine, "dp", axis=0, tiled=True)

    def send_part(part):
        summed = lax.psum_scatter(part, "dp", scatter_dimension=0, tiled=True)
        return lax.all_to_all(summed, "expert", split_axis=0, concat_axis=0, tiled=True)

    rows_x = spread(pick(selector, tokens))
    rows_c = spread(pick(selector, scaled))
    result, grad_gu, grad_down = expert_pass(rows_x, rows_c, w_gu, w_down, send_part)
    grad_tokens = lax.dot_general(selector, result, ROWS, preferred_element_type=F32)
    return grad_tokens.astype(BF16), grad_gu, grad_down


def local(tokens, cotangent, gate, clade, block, plan, w_gu, w_down):
    columns = lax.axis_size("expert")
    groups = lax.axis_size("dp")
    width = tokens.shape[1]
    cap_home = tokens.shape[0] // columns
    cap_guest = tokens.shape[0] // (4 * columns)
    senders = columns * groups
    owner = place(clade, block, plan, columns, cap_home)
    is_home = block < cap_home
    is_guest = (block >= cap_home) & (block < cap_home + cap_guest)
    sel_home = one_hot(columns * cap_home, jnp.where(is_home, owner * cap_home + block, -1))
    sel_guest = one_hot(
        columns * cap_guest, jnp.where(is_guest, owner * cap_guest + block - cap_home, -1)
    )
    scaled = (gate[:, None] * cotangent.astype(F32)).astype(BF16)
    guests = jnp.stack([pick(sel_guest, tokens), pick(sel_guest, scaled)])
    guests = guests.reshape(2, columns, cap_guest, 2, width // 2).transpose(1, 0, 3, 2, 4)
    guests = guests.reshape(columns * 4 * cap_guest, width // 2)
    home_rows = senders * cap_home
    rows_x, rows_c, got = dispatch(
        pick(sel_home, tokens),
        pick(sel_home, scaled),
        guests,
        columns,
        groups,
        home_rows + senders * cap_guest,
    )
    guest_rows = senders * cap_guest
    index = jnp.arange(4 * guest_rows, dtype=jnp.int32)
    piece, row = index // guest_rows, index % guest_rows
    source = (row // cap_guest) * (4 * cap_guest) + piece * cap_guest + row % cap_guest
    got = pick(one_hot(4 * guest_rows, source).T, got)
    for piece, at in ((0, 0), (1, width // 2)):
        lower = got[piece * guest_rows : (piece + 1) * guest_rows]
        rows_x = lax.dynamic_update_slice(rows_x, lower, (home_rows, at))
        upper = got[(piece + 2) * guest_rows : (piece + 3) * guest_rows]
        rows_c = lax.dynamic_update_slice(rows_c, upper, (home_rows, at))

    def send_part(part):
        thin = part[home_rows:].reshape(senders, cap_guest, 4, width // 4).transpose(0, 2, 1, 3)
        return give_back(part, thin.reshape(senders * 4 * cap_guest, width // 4), columns, groups)

    (home, thin), grad_gu, grad_down = expert_pass(rows_x, rows_c, w_gu, w_down, send_part)
    thin = thin.reshape(columns, 4, cap_guest, width // 4).transpose(0, 2, 1, 3)
    thin = thin.reshape(columns * cap_guest, width)
    result = lax.dot_general(sel_home, home, ROWS, preferred_element_type=F32)
    result = result + lax.dot_general(sel_guest, thin, ROWS, preferred_element_type=F32)
    return result.astype(BF16), grad_gu, grad_down


def solution(mesh):
    placed = (
        P(("dp", "expert"), None),
        P(("dp", "expert"), None),
        P(("dp", "expert")),
        P(("dp", "expert")),
        P(("dp", "expert")),
        P(),
        P("expert", None, "dp", None),
        P("expert", "dp", None),
    )

    def run(*arrays):
        columns = mesh.shape["expert"]
        each = arrays[0].shape[0] // mesh.size
        whole_blocks = each == 16 * columns and mesh.shape["dp"] == 4
        return jax.shard_map(
            local if whole_blocks else local_general,
            mesh=mesh,
            in_specs=placed,
            out_specs=(
                P(("dp", "expert"), None),
                P("expert", None, "dp", None),
                P("expert", "dp", None),
            ),
            check_vma=False,
        )(*arrays)

    return run
```

```python
import functools

import jax
import jax.numpy as jnp
from jax import lax
from jax.experimental import pallas as pl
from jax.experimental.pallas import tpu as pltpu
from jax.sharding import PartitionSpec as P

F32 = jnp.float32
BF16 = jnp.bfloat16
MESH = pl.DeviceIdType.MESH
LAST = (((1,), (1,)), ((), ()))
ROWS = (((0,), (0,)), ((), ()))


def one_hot(count, index):
    return (jnp.arange(count, dtype=jnp.int32)[:, None] == index[None, :]).astype(BF16)


def place(clade, block, plan, columns, cap_home):
    experts = plan.shape[0]
    matches = clade[:, None] == jnp.arange(experts, dtype=jnp.int32)[None, :]
    lookup = jnp.sum(jnp.where(matches, plan[None, :], 0), axis=1)
    return jnp.where(block < cap_home, clade, (lookup + columns // 2) % columns)


def flipped(index, mask, columns):
    total = 0
    bit = 1
    while bit < columns:
        total = total + lax.rem(lax.div(index, bit) + (mask // bit) % 2, 2) * bit
        bit *= 2
    return total


def peers(columns, groups):
    d = lax.axis_index("dp")
    e = lax.axis_index("expert")
    core = d + 1 - 2 * lax.rem(d, 2)
    across = lax.rem(d + 2, groups)
    return d, e, core, across, core + 2 - 4 * (core // 2)


def greet(d, e, core, across, columns):
    barrier = pltpu.get_barrier_semaphore()
    for mask in range(1, columns):
        pl.semaphore_signal(
            barrier, inc=1, device_id=(d, flipped(e, mask, columns)), device_id_type=MESH
        )
    pl.semaphore_signal(barrier, inc=1, device_id=(core, e), device_id_type=MESH)
    pl.semaphore_signal(barrier, inc=1, device_id=(across, e), device_id_type=MESH)
    pl.semaphore_wait(barrier, columns + 1)


def dispatch_kernel(columns, groups, *refs):
    sources = refs[:3]
    outs = refs[3:6]
    local_sem, send_a, send_core, send_x, send_fwd, recv = refs[6:]
    d, e, core, across, diagonal = peers(columns, groups)
    greet(d, e, core, across, columns)
    half = columns // 2
    near = [flipped(e, mask, columns) for mask in range(columns)]
    sends = [mask for pair in zip(range(1, half + 1), range(half, columns)) for mask in pair]
    sends = list(dict.fromkeys(sends))
    kinds = range(3)

    def rows(index):
        return pl.ds(pl.multiple_of(index * 16, 16), 16)

    def remote(k, source, slot, send_sem, target):
        return pltpu.make_async_remote_copy(
            src_ref=source,
            dst_ref=outs[k].at[rows(slot)],
            send_sem=send_sem,
            recv_sem=recv.at[slot, k],
            device_id=target,
            device_id_type=MESH,
        )

    def arrived(k, slot):
        pltpu.make_async_copy(outs[k].at[rows(slot)], outs[k].at[rows(slot)], recv.at[slot, k]).wait()

    copies = []
    local = []
    mine = d * columns + e
    for k in kinds:
        own = sources[k].at[rows(e)]
        copies.append(remote(k, own, mine, send_x.at[0, k], (across, e)))
        copies[-1].start()
    for mask in sends:
        target = near[mask]
        for k in kinds:
            source = sources[k].at[rows(target)]
            copies.append(remote(k, source, mine, send_a.at[mask, k], (d, target)))
            copies[-1].start()
    for k in kinds:
        own = sources[k].at[rows(e)]
        copies.append(remote(k, own, mine, send_core.at[0, k], (core, e)))
        copies[-1].start()
    for k in kinds:
        copy = pltpu.make_async_copy(sources[k].at[rows(e)], outs[k].at[rows(mine)], local_sem.at[k])
        copy.start()
        local.append(copy)
    for i in range(columns + 2):
        if 0 < i < columns:
            slot = d * columns + near[i]
            for k in kinds:
                arrived(k, slot)
                block = outs[k].at[rows(slot)]
                copies.append(remote(k, block, slot, send_x.at[i, k], (across, e)))
                copies[-1].start()
                copies.append(remote(k, block, slot, send_core.at[i, k], (core, e)))
                copies[-1].start()
        if i > 1:
            slot = across * columns + near[i - 2]
            for k in kinds:
                arrived(k, slot)
                block = outs[k].at[rows(slot)]
                copies.append(remote(k, block, slot, send_fwd.at[i - 2, k], (core, e)))
                copies[-1].start()
    for group in (core, diagonal):
        for i in range(columns):
            slot = group * columns + near[i]
            for k in kinds:
                arrived(k, slot)
    for copy in local:
        copy.wait()
    for copy in copies:
        copy.wait_send()


def dispatch(send_x, send_c, send_g, columns, groups, row_count):
    width = send_x.shape[1]
    senders = columns * groups
    sem = pltpu.SemaphoreType.DMA
    return pl.pallas_call(
        functools.partial(dispatch_kernel, columns, groups),
        out_shape=(
            jax.ShapeDtypeStruct((row_count, width), BF16),
            jax.ShapeDtypeStruct((row_count, width), BF16),
            jax.ShapeDtypeStruct((senders * 16, width // 2), BF16),
        ),
        in_specs=[pl.BlockSpec(memory_space=pl.ANY)] * 3,
        out_specs=(pl.BlockSpec(memory_space=pl.ANY),) * 3,
        scratch_shapes=[
            sem((3,)),
            sem((columns, 3)),
            sem((columns, 3)),
            sem((columns, 3)),
            sem((columns, 3)),
            sem((senders, 3)),
        ],
        compiler_params=pltpu.CompilerParams(collective_id=0, has_side_effects=True),
        name="dispatch",
    )(send_x, send_c, send_g)


def return_kernel(columns, groups, part_h, part_g, out_h, out_g, *scratch):
    pair_in = scratch[0:2]
    pair_out = scratch[2:4]
    cross_in = scratch[4:6]
    final = scratch[6:8]
    send_core, send_x, send_a, recv_core, recv_x, recv_a = scratch[8:]
    parts = (part_h, part_g)
    outs = (out_h, out_g)
    d, e, core, across, diagonal = peers(columns, groups)
    greet(d, e, core, across, columns)
    half = columns // 2
    ahead = half
    order = list(range(half, columns)) + list(range(half - 1, -1, -1))
    order = [flipped(e, mask, columns) for mask in order]
    kinds = range(2)

    def rows(index):
        return pl.ds(pl.multiple_of(index * 16, 16), 16)

    copies = []
    core_in = {}

    def to_core(side, group):
        for i in range(columns):
            s = order[i]
            for k in kinds:
                place_in = pair_in[k].at[rows(side * columns + s)]
                copy = pltpu.make_async_remote_copy(
                    src_ref=parts[k].at[rows(group * columns + s)],
                    dst_ref=place_in,
                    send_sem=send_core.at[side, i, k],
                    recv_sem=recv_core.at[side, i, k],
                    device_id=(core, e),
                    device_id_type=MESH,
                )
                copy.start()
                copies.append(copy)
                core_in[side, i, k] = copy

    to_core(0, diagonal)
    cross = {}
    back = {}

    def finish(i):
        s = order[i]
        for k in kinds:
            core_in[1, i, k].wait_recv()
            cross[i, k].wait_recv()
            final[k][rows(s)] = (
                parts[k][rows(d * columns + s)].astype(F32)
                + pair_in[k][rows(columns + s)].astype(F32)
                + cross_in[k][rows(s)].astype(F32)
            ).astype(BF16)
            if i == columns - 1:
                outs[k][rows(e)] = final[k][rows(s)]
            else:
                copy = pltpu.make_async_remote_copy(
                    src_ref=final[k].at[rows(s)],
                    dst_ref=outs[k].at[rows(e)],
                    send_sem=send_a.at[i, k],
                    recv_sem=recv_a.at[i, k],
                    device_id=(d, s),
                    device_id_type=MESH,
                )
                copy.start()
                copies.append(copy)
                back[i, k] = copy

    for i in range(columns):
        s = order[i]
        for k in kinds:
            core_in[0, i, k].wait_recv()
            pair_out[k][rows(s)] = (
                parts[k][rows(across * columns + s)].astype(F32)
                + pair_in[k][rows(s)].astype(F32)
            ).astype(BF16)
            copy = pltpu.make_async_remote_copy(
                src_ref=pair_out[k].at[rows(s)],
                dst_ref=cross_in[k].at[rows(s)],
                send_sem=send_x.at[i, k],
                recv_sem=recv_x.at[i, k],
                device_id=(across, e),
                device_id_type=MESH,
            )
            copy.start()
            copies.append(copy)
            cross[i, k] = copy
        if i == 0:
            to_core(1, core)
        if i >= ahead:
            finish(i - ahead)
    for i in range(columns - ahead, columns):
        finish(i)
    for copy in back.values():
        copy.wait_recv()
    for copy in copies:
        copy.wait_send()


def give_back(part, part_g, columns, groups):
    width = part.shape[1]
    thin = part_g.shape[1]
    sem = pltpu.SemaphoreType.DMA
    vmem = pl.BlockSpec(memory_space=pltpu.VMEM)
    scratch = []
    for count in (2 * columns, columns, columns, columns):
        for wide in (width, thin):
            scratch.append(pltpu.VMEM((count * 16, wide), BF16))
    return pl.pallas_call(
        functools.partial(return_kernel, columns, groups),
        out_shape=(
            jax.ShapeDtypeStruct((columns * 16, width), BF16),
            jax.ShapeDtypeStruct((columns * 16, thin), BF16),
        ),
        in_specs=[vmem, vmem],
        out_specs=(vmem, vmem),
        scratch_shapes=scratch
        + [
            sem((2, columns, 2)),
            sem((columns, 2)),
            sem((columns, 2)),
            sem((2, columns, 2)),
            sem((columns, 2)),
            sem((columns, 2)),
        ],
        compiler_params=pltpu.CompilerParams(
            collective_id=1, has_side_effects=True, vmem_limit_bytes=48 * 2**20
        ),
        name="give_back",
    )(part, part_g)


def expert_pass(rows_x, rows_c, w_gu, w_down, send_part):
    units = w_gu.shape[2]
    both_w = w_gu.reshape(2 * units, w_gu.shape[3])
    pre = lax.dot_general(rows_x, both_w, LAST, preferred_element_type=F32)
    gate_pre, up_pre = pre[:, :units], pre[:, units:]
    hidden_cot = lax.dot_general(rows_c, w_down[0], LAST, preferred_element_type=F32)
    sigmoid = jax.nn.sigmoid(gate_pre)
    hidden = (gate_pre * sigmoid * up_pre).astype(BF16)
    up_cot = (hidden_cot * gate_pre * sigmoid).astype(BF16)
    gate_cot = (hidden_cot * up_pre * sigmoid * (1.0 + gate_pre * (1.0 - sigmoid))).astype(BF16)
    both_cot = jnp.concatenate([gate_cot, up_cot], axis=1)
    part = jnp.dot(both_cot, both_w, preferred_element_type=F32).astype(BF16)
    result = send_part(part)
    d_both = lax.dot_general(both_cot, rows_x, ROWS, preferred_element_type=F32)
    d_down = lax.dot_general(hidden, rows_c, ROWS, preferred_element_type=F32)
    return result, d_both.astype(BF16).reshape(w_gu.shape), d_down.astype(BF16)[None]


def pick(selector, rows):
    return jnp.dot(selector, rows, preferred_element_type=F32).astype(BF16)


def local_general(tokens, cotangent, gate, clade, block, plan, w_gu, w_down):
    columns = lax.axis_size("expert")
    cap_home = tokens.shape[0] // columns
    cap_rows = cap_home + tokens.shape[0] // (4 * columns)
    owner = place(clade, block, plan, columns, cap_home)
    slot = jnp.where(block < cap_rows, owner * cap_rows + block, -1)
    selector = one_hot(columns * cap_rows, slot)
    scaled = (gate[:, None] * cotangent.astype(F32)).astype(BF16)

    def spread(rows):
        mine = lax.all_to_all(rows, "expert", split_axis=0, concat_axis=0, tiled=True)
        return lax.all_gather(mine, "dp", axis=0, tiled=True)

    def send_part(part):
        summed = lax.psum_scatter(part, "dp", scatter_dimension=0, tiled=True)
        return lax.all_to_all(summed, "expert", split_axis=0, concat_axis=0, tiled=True)

    rows_x = spread(pick(selector, tokens))
    rows_c = spread(pick(selector, scaled))
    result, grad_gu, grad_down = expert_pass(rows_x, rows_c, w_gu, w_down, send_part)
    grad_tokens = lax.dot_general(selector, result, ROWS, preferred_element_type=F32)
    return grad_tokens.astype(BF16), grad_gu, grad_down


def local(tokens, cotangent, gate, clade, block, plan, w_gu, w_down):
    columns = lax.axis_size("expert")
    groups = lax.axis_size("dp")
    width = tokens.shape[1]
    cap_home = tokens.shape[0] // columns
    cap_guest = tokens.shape[0] // (4 * columns)
    senders = columns * groups
    owner = place(clade, block, plan, columns, cap_home)
    is_home = block < cap_home
    is_guest = (block >= cap_home) & (block < cap_home + cap_guest)
    sel_home = one_hot(columns * cap_home, jnp.where(is_home, owner * cap_home + block, -1))
    sel_guest = one_hot(
        columns * cap_guest, jnp.where(is_guest, owner * cap_guest + block - cap_home, -1)
    )
    scaled = (gate[:, None] * cotangent.astype(F32)).astype(BF16)
    guests = jnp.stack([pick(sel_guest, tokens), pick(sel_guest, scaled)])
    guests = guests.reshape(2, columns, cap_guest, 2, width // 2).transpose(1, 0, 3, 2, 4)
    guests = guests.reshape(columns * 4 * cap_guest, width // 2)
    home_rows = senders * cap_home
    rows_x, rows_c, got = dispatch(
        pick(sel_home, tokens),
        pick(sel_home, scaled),
        guests,
        columns,
        groups,
        home_rows + senders * cap_guest,
    )
    guest_rows = senders * cap_guest
    index = jnp.arange(4 * guest_rows, dtype=jnp.int32)
    piece, row = index // guest_rows, index % guest_rows
    source = (row // cap_guest) * (4 * cap_guest) + piece * cap_guest + row % cap_guest
    got = pick(one_hot(4 * guest_rows, source).T, got)
    for piece, at in ((0, 0), (1, width // 2)):
        lower = got[piece * guest_rows : (piece + 1) * guest_rows]
        rows_x = lax.dynamic_update_slice(rows_x, lower, (home_rows, at))
        upper = got[(piece + 2) * guest_rows : (piece + 3) * guest_rows]
        rows_c = lax.dynamic_update_slice(rows_c, upper, (home_rows, at))

    def send_part(part):
        thin = part[home_rows:].reshape(senders, cap_guest, 4, width // 4).transpose(0, 2, 1, 3)
        return give_back(part, thin.reshape(senders * 4 * cap_guest, width // 4), columns, groups)

    (home, thin), grad_gu, grad_down = expert_pass(rows_x, rows_c, w_gu, w_down, send_part)
    thin = thin.reshape(columns, 4, cap_guest, width // 4).transpose(0, 2, 1, 3)
    thin = thin.reshape(columns * cap_guest, width)
    result = lax.dot_general(sel_home, home, ROWS, preferred_element_type=F32)
    result = result + lax.dot_general(sel_guest, thin, ROWS, preferred_element_type=F32)
    return result.astype(BF16), grad_gu, grad_down


def solution(mesh):
    placed = (
        P(("dp", "expert"), None),
        P(("dp", "expert"), None),
        P(("dp", "expert")),
        P(("dp", "expert")),
        P(("dp", "expert")),
        P(),
        P("expert", None, "dp", None),
        P("expert", "dp", None),
    )

    def run(*arrays):
        columns = mesh.shape["expert"]
        each = arrays[0].shape[0] // mesh.size
        whole_blocks = each == 16 * columns and mesh.shape["dp"] == 4
        return jax.shard_map(
            local if whole_blocks else local_general,
            mesh=mesh,
            in_specs=placed,
            out_specs=(
                P(("dp", "expert"), None),
                P("expert", None, "dp", None),
                P("expert", "dp", None),
            ),
            check_vma=False,
        )(*arrays)

    return run
```
